128 devices in a mesh: seq: 64 (over y, x, z), head: 2 (over core).
Axes of the slice: x: 4, y: 4, z: 4, core: 2. Of those that a mesh axis runs over, the one named last changes fastest.
Arguments:
- queries: bfloat16 [32768, 512], P('seq', 'head'), may hold values from -420 to 420
- key_vectors: bfloat16 [32768, 512], P('seq', 'head'), may hold values from -10 to 10
- value_vectors: bfloat16 [32768, 512], P('seq', 'head'), may hold values from -6 to 6
- out_weight: bfloat16 [512, 1024], P('head'), may hold values from -0.25 to 0.25
- out_grad: bfloat16 [32768, 1024], P('seq'), may hold values from -6 to 6
Outputs:
- mixed: bfloat16 [32768, 1024], P('seq', 'head')
- query_grads: bfloat16 [32768, 512], P('seq', 'head')
- key_grads: bfloat16 [32768, 512], P('seq', 'head')
- value_grads: bfloat16 [32768, 512], P('seq', 'head')
The draws below stay inside these ranges and needn't reach their ends.
All inputs are finite; a program needn't handle non-finite values.
Results may differ from the reference program's by a relative error of at most 0.035.
Values may be sent and summed in bfloat16 or wider, within the bound.
No kernel may reach another device: no remote copies, remote signals or barrier semaphores. Data moves between devices by JAX's collectives and lax.ppermute only.
A program may use at most 192 MiB of HBM per device.

```python
import math
import jax
import jax.numpy as jnp
from jax import lax

D = 1024
HEADS = 8
HEAD_DIM = 64
BLOCK = 512
TOKENS = 32768
LEVELS = 6
N_SEQ = 64


def twin_table(key):
    base_table = jax.random.normal(key, (TOKENS, HEADS * HEAD_DIM), jnp.float32)
    row_index = jnp.arange(TOKENS)
    twin_rows = (row_index % 64 == 6)[:, None]
    return jnp.where(twin_rows, base_table, base_table)


def draw_key_vectors(key, part):
    table = twin_table(key)
    row_index = jnp.arange(TOKENS)
    boosted_rows = ((row_index % 64 == 5) | (row_index % 64 == 6))[:, None]
    scaled = jnp.where(boosted_rows, jnp.clip(table, -10.0, 10.0), table)
    return scaled.astype(jnp.bfloat16)


def draw_queries(key, part):
    key = jax.random.fold_in(key, 5)
    fresh = jax.random.normal(key, (TOKENS, HEADS * HEAD_DIM), jnp.float32)
    aligned = (jnp.arange(TOKENS) % 64 == 5)[:, None]
    return jnp.where(aligned, fresh, fresh).astype(jnp.bfloat16)


def steps_of(own_key, shape, split, low, high):
    gain, own = 1.0, jax.random.fold_in(own_key, 6)
    for dim, shards_of in split:
        draws = jnp.exp(jax.random.uniform(jax.random.fold_in(own, dim), (shards_of,), jnp.float32, low / len(split), high / len(split)))
        gain = gain * jnp.repeat(draws, shape[dim] // shards_of).reshape([-1 if axis == dim else 1 for axis in range(len(shape))])
    return gain


def noise(own_key, extent, width, bound, cuts=(), kind=jnp.bfloat16):
    array = width * jax.random.normal(own_key, extent, jnp.float32)
    if cuts:
        array = array * steps_of(own_key, extent, cuts, -0.22, 0.18)
    return jnp.clip(array, -bound, bound).astype(kind)


def setup_inputs(seed: int = 0) -> dict:
    arg_keys = jax.random.split(jax.random.key(seed), 6)
    queries = draw_queries(jax.random.fold_in(arg_keys[5], 71), 0)
    key_vectors = draw_key_vectors(jax.random.fold_in(arg_keys[5], 71), 0)
    value_vectors = noise(arg_keys[2], (TOKENS, HEADS * HEAD_DIM), 1.0, 6.0, ((0, 64), (1, 2)))
    out_weight = noise(arg_keys[3], (HEADS * HEAD_DIM, D), (HEADS * HEAD_DIM) ** -0.5, 0.25, ((0, 2),))
    out_grad = noise(arg_keys[4], (TOKENS, D), 1.0, 6.0, ((0, 64),))
    return {"queries": queries, "key_vectors": key_vectors, "value_vectors": value_vectors, "out_weight": out_weight, "out_grad": out_grad}


def pair_mean(table_in):
    widened = table_in.astype(jnp.float32)
    return ((widened[0::2] + widened[1::2]) * 0.5).astype(jnp.bfloat16)


def level_scores(query_heads, key_heads, scale_factor, level_now):
    raw_scores = jnp.einsum('qhd,khd->hqk', query_heads.astype(jnp.float32), key_heads.astype(jnp.float32))
    return raw_scores * scale_factor + max(level_now - 1, 0) * math.log(2.0)


def block_pass(query_heads, key_list, value_list, grad_rows, out_weight, scale_factor):
    head_count = query_heads.shape[1]
    block_rows = query_heads.shape[0]
    running_top = jnp.full((head_count, block_rows), -jnp.inf, jnp.float32)
    running_total = jnp.zeros((head_count, block_rows), jnp.float32)
    running_acc = jnp.zeros((head_count, block_rows, HEAD_DIM), jnp.float32)
    for level_now in range(len(key_list)):
        score_now = level_scores(query_heads, key_list[level_now], scale_factor, level_now)
        new_top = jnp.maximum(running_top, jnp.max(score_now, axis=2))
        shrink = jnp.exp(running_top - new_top)
        probs = jnp.exp(score_now - new_top[:, :, None]).astype(jnp.bfloat16).astype(jnp.float32)
        running_total = running_total * shrink + jnp.sum(probs, axis=2)
        running_acc = running_acc * shrink[:, :, None] + jnp.einsum('hqk,khd->hqd', probs, value_list[level_now].astype(jnp.float32))
        running_top = new_top
    attended = jnp.transpose(running_acc / running_total[:, :, None], (1, 0, 2)).astype(jnp.bfloat16)
    log_total = running_top + jnp.log(running_total)
    attended_rows = attended.reshape(block_rows, head_count * HEAD_DIM)
    d_att = jnp.dot(grad_rows, out_weight.T, preferred_element_type=jnp.float32).astype(jnp.bfloat16)
    d_heads = d_att.reshape(block_rows, head_count, HEAD_DIM).astype(jnp.float32)
    delta = jnp.transpose(jnp.sum(d_heads * attended.astype(jnp.float32), axis=2))
    query_acc = jnp.zeros((block_rows, head_count, HEAD_DIM), jnp.float32)
    key_parts = []
    value_parts = []
    for level_now in range(len(key_list)):
        key_now = key_list[level_now].astype(jnp.float32)
        value_now = value_list[level_now].astype(jnp.float32)
        score_now = level_scores(query_heads, key_list[level_now], scale_factor, level_now)
        back_probs = jnp.exp(score_now - log_total[:, :, None]).astype(jnp.bfloat16).astype(jnp.float32)
        value_parts.append(jnp.einsum('hqk,qhd->khd', back_probs, d_heads))
        prob_grads = jnp.einsum('qhd,khd->hqk', d_heads, value_now)
        score_grads = (back_probs * (prob_grads - delta[:, :, None])).astype(jnp.bfloat16).astype(jnp.float32)
        query_acc = query_acc + jnp.einsum('hqk,khd->qhd', score_grads, key_now) * scale_factor
        key_parts.append(jnp.einsum('hqk,qhd->khd', score_grads, query_heads.astype(jnp.float32)) * scale_factor)
    feat_width = head_count * HEAD_DIM
    key_stack = jnp.stack([part.reshape(block_rows, feat_width) for part in key_parts])
    value_stack = jnp.stack([part.reshape(block_rows, feat_width) for part in value_parts])
    return attended_rows, query_acc.reshape(block_rows, feat_width).astype(jnp.bfloat16), key_stack, value_stack


def fold_back(level_grads):
    feat_width = HEADS * HEAD_DIM
    carried = None
    for level_now in range(LEVELS, 0, -1):
        group_size = 2 ** (level_now - 1)
        span_count = N_SEQ // group_size
        grouped = jnp.sum(level_grads[:, level_now].reshape(span_count, group_size, BLOCK, feat_width), axis=1)
        span_ids = jnp.bitwise_xor(jnp.arange(span_count, dtype=jnp.int32), 1)
        landed = jnp.take(grouped, span_ids, axis=0).reshape(span_count * BLOCK, feat_width)
        if carried is not None:
            landed = landed + 0.5 * jnp.repeat(carried, 2, axis=0)
        carried = landed
    return level_grads[:, 0].reshape(TOKENS, feat_width) + carried


def reference(queries, key_vectors, value_vectors, out_weight, out_grad):
    feat_width = HEADS * HEAD_DIM
    scale_factor = HEAD_DIM ** -0.5
    key_levels = [key_vectors]
    value_levels = [value_vectors]
    for level_now in range(1, LEVELS):
        key_levels.append(pair_mean(key_levels[-1]))
        value_levels.append(pair_mean(value_levels[-1]))
    block_ids = jnp.arange(N_SEQ, dtype=jnp.int32)
    far_keys = []
    far_values = []
    for level_now in range(1, LEVELS + 1):
        span_count = N_SEQ // 2 ** (level_now - 1)
        partner_ids = jnp.bitwise_xor(jnp.right_shift(block_ids, level_now - 1), 1)
        far_keys.append(jnp.take(key_levels[level_now - 1].reshape(span_count, BLOCK, feat_width), partner_ids, axis=0))
        far_values.append(jnp.take(value_levels[level_now - 1].reshape(span_count, BLOCK, feat_width), partner_ids, axis=0))
    far_keys = jnp.stack(far_keys, axis=1)
    far_values = jnp.stack(far_values, axis=1)

    def per_block(inputs):
        query_rows, key_rows, value_rows, grad_rows, far_key_rows, far_value_rows = inputs
        query_heads = query_rows.reshape(BLOCK, HEADS, HEAD_DIM)
        key_list = [key_rows.reshape(BLOCK, HEADS, HEAD_DIM)] + [far_key_rows[index].reshape(BLOCK, HEADS, HEAD_DIM) for index in range(LEVELS)]
        value_list = [value_rows.reshape(BLOCK, HEADS, HEAD_DIM)] + [far_value_rows[index].reshape(BLOCK, HEADS, HEAD_DIM) for index in range(LEVELS)]
        return block_pass(query_heads, key_list, value_list, grad_rows, out_weight, scale_factor)

    results = lax.map(per_block, (queries.reshape(N_SEQ, BLOCK, feat_width), key_vectors.reshape(N_SEQ, BLOCK, feat_width), value_vectors.reshape(N_SEQ, BLOCK, feat_width), out_grad.reshape(N_SEQ, BLOCK, D), far_keys, far_values))
    attended = results[0].reshape(TOKENS, feat_width)
    mixed = jnp.dot(attended, out_weight, preferred_element_type=jnp.float32).astype(jnp.bfloat16)
    query_grads = results[1].reshape(TOKENS, feat_width)
    key_grads = fold_back(results[2]).astype(jnp.bfloat16)
    value_grads = fold_back(results[3]).astype(jnp.bfloat16)
    return mixed, query_grads, key_grads, value_grads
```

```python
import math

import jax
import jax.numpy as jnp
from jax import lax
from jax.experimental import pallas as pl
from jax.experimental.pallas import tpu as pltpu
from jax.sharding import PartitionSpec as P

HEAD_DIM = 64
ROWS = 512
FEAT = 256
HEADS = 4
PAIR = 2 * FEAT
LN2 = math.log(2.0)
F32 = jnp.float32
BF16 = jnp.bfloat16
NT = (((1,), (1,)), ((), ()))
VMEM_LIMIT = 48 * 1024 * 1024


def call(body, outs, args, name, flops=0, scratch=(), smem=()):
    in_specs = [
        pl.BlockSpec(memory_space=pltpu.SMEM if i in smem else pltpu.VMEM)
        for i in range(len(args))
    ]
    moved = sum(math.prod(s) * jnp.dtype(t).itemsize for s, t in outs)
    moved += sum(math.prod(a.shape) * a.dtype.itemsize for a in args)
    return pl.pallas_call(
        body,
        out_shape=[jax.ShapeDtypeStruct(s, t) for s, t in outs],
        in_specs=in_specs,
        out_specs=[pl.BlockSpec(memory_space=pltpu.VMEM) for _ in outs],
        scratch_shapes=list(scratch),
        compiler_params=pltpu.CompilerParams(vmem_limit_bytes=VMEM_LIMIT),
        cost_estimate=pl.CostEstimate(flops=flops, bytes_accessed=moved, transcendentals=0),
        name=name,
    )(*args)


def dot(a, b):
    return jnp.dot(a, b, preferred_element_type=F32)


def dot_nt(a, b):
    return lax.dot_general(a, b, NT, preferred_element_type=F32)


def pair_matrix(rows, fold, weight):
    r = lax.broadcasted_iota(jnp.int32, (rows, rows * fold), 0)
    c = lax.broadcasted_iota(jnp.int32, (rows, rows * fold), 1)
    return jnp.where(c // fold == r, weight, 0.0).astype(BF16)


def spread_matrix(rows, fold, weight):
    r = lax.broadcasted_iota(jnp.int32, (rows * fold, rows), 0)
    c = lax.broadcasted_iota(jnp.int32, (rows * fold, rows), 1)
    return jnp.where(r // fold == c, weight, 0.0).astype(BF16)


def halve(x):
    return dot(pair_matrix(x.shape[0] // 2, 2, 0.5), x).astype(BF16)


def head_mask(head, value):
    lane = lax.broadcasted_iota(jnp.int32, (1, FEAT), 1)
    return jnp.where(lane // HEAD_DIM == head, value, 0.0).astype(BF16)


def prep_body(k_ref, v_ref, kv_ref, c2_ref, c3_ref):
    kv_ref[:, :FEAT] = k_ref[...]
    kv_ref[:, FEAT:] = v_ref[...]
    c2_ref[...] = halve(kv_ref[...])
    c3_ref[...] = halve(c2_ref[...])


def gather_body(place_ref, own_ref, a_ref, b_ref, c_ref, whole_ref, half_ref, quarter_ref=None):
    place = place_ref[0]
    for mask, ref in ((0, own_ref), (1, a_ref), (2, b_ref), (3, c_ref)):
        at = pl.multiple_of(jnp.bitwise_xor(place, mask) * 128, 128)
        whole_ref[pl.ds(at, 128), :] = ref[...]
    half_ref[...] = halve(whole_ref[...])
    if quarter_ref is not None:
        quarter_ref[...] = halve(half_ref[...])


def forward_chunks(q, chunks, state_in, state_out):
    top_out, acc_out = state_out
    ones = jnp.ones((16, ROWS), BF16)
    flipped = [ref[:, FEAT:].T for ref, _ in chunks]
    for head in range(HEADS):
        qh = q * head_mask(head, HEAD_DIM**-0.5)
        scores = [dot_nt(ref[:, :FEAT], qh) for ref, _ in chunks]
        tops = [jnp.max(s, axis=0, keepdims=True) + bias for s, (_, bias) in zip(scores, chunks)]
        top = tops[0]
        for other in tops[1:]:
            top = jnp.maximum(top, other)
        if state_in is not None:
            old = state_in[0][head : head + 1, :]
            top = jnp.maximum(top, old)
            acc = state_in[1][head] * jnp.exp(old - top)
        else:
            acc = None
        for s, (ref, bias), vt in zip(scores, chunks, flipped):
            p = jnp.exp(s + (bias - top)).astype(BF16)
            rows = ref.shape[0]
            vh = jnp.concatenate(
                [vt[head * HEAD_DIM : (head + 1) * HEAD_DIM, :], ones[:, :rows]], axis=0
            )
            add = dot(vh, p)
            acc = add if acc is None else acc + add
        top_out[head : head + 1, :] = top
        acc_out[head] = acc


def forward_body(biases, has_state, *refs):
    n = len(biases)
    q_ref, chunks, rest = refs[0], refs[1 : 1 + n], refs[1 + n :]
    state_in = rest[:2] if has_state else None
    state_out = rest[2:4] if has_state else rest[:2]
    forward_chunks(q_ref[...], list(zip(chunks, biases)), state_in, state_out)


def run_forward(q, chunks, biases, state, name):
    args = [q, *chunks] + ([] if state is None else list(state))
    keys = sum(c.shape[0] for c in chunks)
    return call(
        lambda *refs: forward_body(biases, state is not None, *refs),
        [((8, ROWS), F32), ((HEADS, 80, ROWS), F32)],
        args,
        name,
        flops=2 * 2 * 4 * keys * ROWS * FEAT,
    )


def grad_in_body(og_ref, w_ref, d_ref, dt_ref):
    d_ref[...] = dot_nt(og_ref[...], w_ref[...]).astype(BF16)
    dt_ref[...] = dot_nt(w_ref[...], og_ref[...]).astype(BF16)


def finish_body(biases, *refs):
    n = len(biases)
    q_ref, chunks, rest = refs[0], refs[1 : 1 + n], refs[1 + n :]
    top_in, acc_in, dt_ref, att_ref, stat_ref, top_s, acc_s = rest
    forward_chunks(q_ref[...], list(zip(chunks, biases)), (top_in, acc_in), (top_s, acc_s))
    pieces = []
    for head in range(HEADS):
        den = acc_s[head, HEAD_DIM : HEAD_DIM + 1, :]
        att = (acc_s[head, :HEAD_DIM, :] / den).astype(BF16)
        pieces.append(att)
        dh = dt_ref[head * HEAD_DIM : (head + 1) * HEAD_DIM, :].astype(F32)
        stat_ref[head : head + 1, :] = top_s[head : head + 1, :] + jnp.log(den)
        stat_ref[HEADS + head : HEADS + head + 1, :] = jnp.sum(
            dh * att.astype(F32), axis=0, keepdims=True
        )
    att_ref[...] = jnp.concatenate(pieces, axis=0).T


def run_finish(q, chunks, biases, state, dt):
    keys = sum(c.shape[0] for c in chunks)
    return call(
        lambda *refs: finish_body(biases, *refs),
        [((ROWS, FEAT), BF16), ((8, ROWS), F32)],
        [q, *chunks, *state, dt],
        "finish",
        flops=2 * 2 * 4 * keys * ROWS * FEAT,
        scratch=[pltpu.VMEM((8, ROWS), F32), pltpu.VMEM((HEADS, 80, ROWS), F32)],
    )


def backward_body(biases, has_acc, last, *refs):
    n = len(biases)
    q_ref, d_ref, stat_ref = refs[:3]
    chunks = refs[3 : 3 + n]
    rest = refs[3 + n :]
    acc_in = rest[0] if has_acc else None
    rest = rest[1:] if has_acc else rest
    outs, dq_ref, qs, ds, ps, gs = rest[:n], rest[n], rest[n + 1], rest[n + 2], rest[n + 3], rest[n + 4]
    q, d = q_ref[...], d_ref[...]
    for head in range(HEADS):
        qs[pl.ds(head * ROWS, ROWS), :] = q * head_mask(head, HEAD_DIM**-0.5)
        ds[pl.ds(head * ROWS, ROWS), :] = d * head_mask(head, 1.0)
    pieces = [None] * HEADS
    for ref, bias, out in zip(chunks, biases, outs):
        rows = ref.shape[0]
        kt = ref[:, :FEAT].T
        for head in range(HEADS):
            at = pl.ds(head * ROWS, ROWS)
            shift = bias - stat_ref[head : head + 1, :]
            delta = stat_ref[HEADS + head : HEADS + head + 1, :]
            s = dot_nt(ref[:, :FEAT], qs[at, :])
            p = jnp.exp(s + shift).astype(BF16)
            ps[:rows, at] = p
            dp = dot_nt(ref[:, FEAT:], ds[at, :])
            g = (p.astype(F32) * (dp - delta)).astype(BF16)
            gs[:rows, at] = g
            part = dot(kt[head * HEAD_DIM : (head + 1) * HEAD_DIM, :], g)
            pieces[head] = part if pieces[head] is None else pieces[head] + part
        out[:, :FEAT] = dot(gs[:rows, :], qs[...]).astype(BF16)
        out[:, FEAT:] = dot(ps[:rows, :], ds[...]).astype(BF16)
    total = jnp.concatenate(pieces, axis=0) * HEAD_DIM**-0.5
    if acc_in is not None:
        total = total + acc_in[...]
    dq_ref[...] = total.T.astype(BF16) if last else total


def run_backward(q, d, stat, chunks, biases, acc, name, last=False):
    args = [q, d, stat, *chunks] + ([] if acc is None else [acc])
    keys = sum(c.shape[0] for c in chunks)
    outs = [((c.shape[0], PAIR), BF16) for c in chunks]
    outs.append(((ROWS, FEAT), BF16) if last else ((FEAT, ROWS), F32))
    return call(
        lambda *refs: backward_body(biases, acc is not None, last, *refs),
        outs,
        args,
        name,
        flops=5 * 2 * 4 * keys * ROWS * FEAT,
        scratch=[
            pltpu.VMEM((HEADS * ROWS, FEAT), BF16),
            pltpu.VMEM((HEADS * ROWS, FEAT), BF16),
            pltpu.VMEM((ROWS, HEADS * ROWS), BF16),
            pltpu.VMEM((ROWS, HEADS * ROWS), BF16),
        ],
    )


def scatter_out(place_ref, total_ref, keep_ref, outs):
    place = place_ref[0]
    for mask, out in zip((1, 2, 3), outs):
        at = pl.multiple_of(jnp.bitwise_xor(place, mask) * 128, 128)
        out[...] = total_ref[pl.ds(at, 128), :].astype(BF16)
    keep_ref[...] = total_ref[pl.ds(pl.multiple_of(place * 128, 128), 128), :]


def home_far_body(place_ref, r_ref, ra_ref, rb_ref, keep_ref, o1_ref, o2_ref, o3_ref, total_ref):
    spread = spread_matrix(256, 2, 0.5)
    total_ref[...] = (
        r_ref[...].astype(F32) + dot(spread, ra_ref[...]) + dot(spread, rb_ref[...])
    )
    scatter_out(place_ref, total_ref, keep_ref, (o1_ref, o2_ref, o3_ref))


def coarse_total(r_ref, ra_ref, rb_ref, kept_ref, e1_ref, e2_ref, e3_ref):
    spread = spread_matrix(256, 2, 0.5)
    below = kept_ref[...] + e1_ref[...].astype(F32) + e2_ref[...].astype(F32)
    below = (below + e3_ref[...].astype(F32)).astype(BF16)
    total = r_ref[...].astype(F32) + dot(spread, ra_ref[...]) + dot(spread, rb_ref[...])
    return total + dot(spread_matrix(128, 4, 0.25), below)


def home_mid_body(
    place_ref, r_ref, ra_ref, rb_ref, kept_ref, e1_ref, e2_ref, e3_ref,
    keep_ref, o1_ref, o2_ref, o3_ref, total_ref,
):
    total_ref[...] = coarse_total(r_ref, ra_ref, rb_ref, kept_ref, e1_ref, e2_ref, e3_ref)
    scatter_out(place_ref, total_ref, keep_ref, (o1_ref, o2_ref, o3_ref))


def home_near_body(
    r_ref, ra_ref, rb_ref, kept_ref, e1_ref, e2_ref, e3_ref, g_ref, dk_ref, dv_ref
):
    total = coarse_total(r_ref, ra_ref, rb_ref, kept_ref, e1_ref, e2_ref, e3_ref)
    total = total + g_ref[...].astype(F32)
    dk_ref[...] = total[:, :FEAT].astype(BF16)
    dv_ref[...] = total[:, FEAT:].astype(BF16)


def mixed_send_body(side_ref, att_ref, w_ref, out_ref):
    at = pl.multiple_of((1 - side_ref[0]) * PAIR, PAIR)
    out_ref[...] = dot(att_ref[...], w_ref[:, pl.ds(at, PAIR)]).astype(BF16)


def mixed_sum_body(side_ref, att_ref, w_ref, got_ref, out_ref):
    at = pl.multiple_of(side_ref[0] * PAIR, PAIR)
    own = dot(att_ref[...], w_ref[:, pl.ds(at, PAIR)])
    out_ref[...] = (own + got_ref[...].astype(F32)).astype(BF16)


def swap(value, mask):
    return lax.ppermute(value, "seq", [(s, s ^ mask) for s in range(lax.axis_size("seq"))])


def after(value, *others):
    return lax.optimization_barrier((value, *others))[0]


def per_device(queries, key_vectors, value_vectors, out_weight, out_grad):
    place = lax.axis_index("seq").astype(jnp.int32)
    side = lax.axis_index("head").astype(jnp.int32).reshape(1)
    place_z = jnp.bitwise_and(place, 3).reshape(1)
    place_x = jnp.bitwise_and(jnp.right_shift(place, 2), 3).reshape(1)
    bias = [max(level - 1, 0) * LN2 for level in range(7)]
    wide, half, part = ((ROWS, PAIR), BF16), ((256, PAIR), BF16), ((128, PAIR), BF16)
    kept = ((128, PAIR), F32)
    whole = pltpu.VMEM((ROWS, PAIR), F32)

    kv, c2, c3 = call(prep_body, [wide, half, part], [key_vectors, value_vectors], "prep")
    s1, s3, s2 = swap(c3, 1), swap(c3, 3), swap(c3, 2)
    d, dt = call(
        grad_in_body, [((ROWS, FEAT), BF16), ((FEAT, ROWS), BF16)], [out_grad, out_weight], "grad_in"
    )
    state = run_forward(queries, [kv], [bias[0]], None, "fwd0")
    own3, c4, c5 = call(
        gather_body, [wide, half, part], [place_z, c3, s1, s2, s3], "gather_z", smem=(0,)
    )
    t1, t3, t2 = swap(c5, 4), swap(c5, 12), swap(c5, 8)
    kv_z, c2_z, _ = lax.optimization_barrier((kv, c2, c5))
    p1, p2a, p2b = swap(kv_z, 1), swap(c2_z, 3), swap(c2_z, 2)
    own5, c6 = call(
        gather_body, [wide, half], [place_x, c5, t1, t2, t3], "gather_x", smem=(0,)
    )
    p5, p6a, p6b = swap(own5, 16), swap(c6, 48), swap(c6, 32)
    own3_x, c4_x, _ = lax.optimization_barrier((own3, c4, c6))
    p3, p4a, p4b = swap(own3_x, 4), swap(c4_x, 12), swap(c4_x, 8)
    state = run_forward(
        queries, [p1, p2a, p2b], [bias[1], bias[2], bias[2]], state, "fwd12"
    )
    state = run_forward(
        queries, [p3, p4a, p4b], [bias[3], bias[4], bias[4]], state, "fwd34"
    )
    att, stat = run_finish(queries, [p5, p6a, p6b], [bias[5], bias[6], bias[6]], state, dt)

    g6a, g6b, dq = run_backward(
        queries, d, stat, [p6a, p6b], [bias[6], bias[6]], None, "bwd6"
    )
    g5, dq = run_backward(queries, d, stat, [p5], [bias[5]], dq, "bwd5")
    r6a, r6b, r5 = swap(g6a, 48), swap(g6b, 32), swap(g5, 16)
    g3, g4a, g4b, dq = run_backward(
        queries, d, stat, [p3, p4a, p4b], [bias[3], bias[4], bias[4]], dq, "bwd34"
    )
    r3, r4a, r4b = swap(g3, 4), swap(g4a, 12), swap(g4b, 8)
    g1, g2a, g2b, dq = run_backward(
        queries, d, stat, [p1, p2a, p2b], [bias[1], bias[2], bias[2]], dq, "bwd12"
    )
    r1, r2a, r2b = swap(g1, 1), swap(g2a, 3), swap(g2b, 2)
    g0, query_grads = run_backward(
        queries, d, stat, [kv], [bias[0]], dq, "bwd0", last=True
    )
    mixed_out = call(
        mixed_send_body, [wide], [side, att, out_weight], "mixed_send", smem=(0,)
    )[0]
    mixed_in = lax.ppermute(mixed_out, "head", [(0, 1), (1, 0)])
    mixed = call(
        mixed_sum_body, [wide], [side, att, out_weight, mixed_in], "mixed_sum", smem=(0,)
    )[0]

    k5, e1, e2, e3 = call(
        home_far_body, [kept, part, part, part], [place_x, r5, r6a, r6b], "home_far",
        scratch=[whole], smem=(0,),
    )
    e1, e3, e2 = swap(e1, 4), swap(e3, 12), swap(e2, 8)
    k3, f1, f2, f3 = call(
        home_mid_body, [kept, part, part, part],
        [place_z, r3, r4a, r4b, k5, e1, e2, e3], "home_mid", scratch=[whole], smem=(0,),
    )
    f1, f3, f2 = swap(f1, 1), swap(f3, 3), swap(f2, 2)
    key_grads, value_grads = call(
        home_near_body, [((ROWS, FEAT), BF16)] * 2, [r1, r2a, r2b, k3, f1, f2, f3, g0], "home_near"
    )
    return (mixed, query_grads, key_grads, value_grads)


def solution(mesh):
    return jax.shard_map(
        per_device,
        mesh=mesh,
        in_specs=(
            P("seq", "head"),
            P("seq", "head"),
            P("seq", "head"),
            P("head", None),
            P("seq", None),
        ),
        out_specs=(P("seq", "head"), P("seq", "head"), P("seq", "head"), P("seq", "head")),
        check_vma=False,
    )
```

```python
import math

import jax
import jax.numpy as jnp
from jax import lax
from jax.experimental import pallas as pl
from jax.experimental.pallas import tpu as pltpu
from jax.sharding import PartitionSpec as P

HEAD_DIM = 64
ROWS = 512
FEAT = 256
HEADS = 4
PAIR = 2 * FEAT
LN2 = math.log(2.0)
F32 = jnp.float32
BF16 = jnp.bfloat16
QB = 256
NT = (((1,), (1,)), ((), ()))
VMEM_LIMIT = 20 * 1024 * 1024
SCALE = 1.0
LIGHT = 0.01
HEAVY = 60.0
TOKEN = ((8, 128), jnp.float32)


def call(body, outs, args, name, us, scratch=(), smem=(), far=(), deps=(), limit=VMEM_LIMIT):
    count = len(args)

    def run(*refs):
        body(*refs[:count], *refs[count + len(deps) :])

    def space(i):
        return pltpu.SMEM if i in smem else pl.ANY if i in far else pltpu.VMEM

    return pl.pallas_call(
        run,
        out_shape=[jax.ShapeDtypeStruct(s, t) for s, t in outs],
        in_specs=[pl.BlockSpec(memory_space=space(i)) for i in range(count)]
        + [pl.BlockSpec(memory_space=pl.ANY)] * len(deps),
        out_specs=[pl.BlockSpec(memory_space=pltpu.VMEM) for _ in outs],
        scratch_shapes=list(scratch),
        compiler_params=pltpu.CompilerParams(vmem_limit_bytes=limit),
        cost_estimate=pl.CostEstimate(
            flops=int(us * SCALE * 1.1e9), bytes_accessed=1 << 16, transcendentals=0
        ),
        name=name,
    )(*args, *deps)


def dot(a, b):
    return jnp.dot(a, b, preferred_element_type=F32)


def dot_nt(a, b):
    return lax.dot_general(a, b, NT, preferred_element_type=F32)


def pair_matrix(rows, fold, weight):
    r = lax.broadcasted_iota(jnp.int32, (rows, rows * fold), 0)
    c = lax.broadcasted_iota(jnp.int32, (rows, rows * fold), 1)
    return jnp.where(c // fold == r, weight, 0.0).astype(BF16)


def spread_matrix(rows, fold, weight):
    r = lax.broadcasted_iota(jnp.int32, (rows * fold, rows), 0)
    c = lax.broadcasted_iota(jnp.int32, (rows * fold, rows), 1)
    return jnp.where(r // fold == c, weight, 0.0).astype(BF16)


def halve(x):
    return dot(pair_matrix(x.shape[0] // 2, 2, 0.5), x).astype(BF16)


def head_mask(head, value):
    lane = lax.broadcasted_iota(jnp.int32, (1, FEAT), 1)
    return jnp.where(lane // HEAD_DIM == head, value, 0.0).astype(BF16)


def prep_body(k_ref, v_ref, kv_ref, c2_ref, c3_ref, sems):
    copies = [
        pltpu.make_async_copy(k_ref, kv_ref.at[:, pl.ds(0, FEAT)], sems.at[0]),
        pltpu.make_async_copy(v_ref, kv_ref.at[:, pl.ds(FEAT, FEAT)], sems.at[1]),
    ]
    for copy in copies:
        copy.start()
    for copy in copies:
        copy.wait()
    c2_ref[...] = halve(kv_ref[...])
    c3_ref[...] = halve(c2_ref[...])


def join_body(own_ref, got_ref, out_ref):
    out_ref[:256, :] = own_ref[...]
    out_ref[256:, :] = halve(got_ref[...])


def gather_body(place_ref, own_ref, a_ref, b_ref, c_ref, whole_ref, half_ref, quarter_ref=None):
    place = place_ref[0]
    for mask, ref in ((0, own_ref), (1, a_ref), (2, b_ref), (3, c_ref)):
        at = pl.multiple_of(jnp.bitwise_xor(place, mask) * 128, 128)
        whole_ref[pl.ds(at, 128), :] = ref[...]
    half_ref[...] = halve(whole_ref[...])
    if quarter_ref is not None:
        quarter_ref[...] = halve(half_ref[...])


def gather_far_body(place_ref, own_ref, a_ref, b_ref, c_ref, whole_ref, half_ref):
    for mask, rows in (
        (0, own_ref[...]),
        (1, halve(halve(a_ref[...]))),
        (2, halve(b_ref[...])),
        (3, halve(c_ref[...])),
    ):
        at = jnp.bitwise_xor(place_ref[0], mask) * 128
        whole_ref[pl.ds(pl.multiple_of(at, 128), 128), :] = rows
    half_ref[...] = halve(whole_ref[...])


def forward_blocks(q, chunks, state_in, state_out, scratch=None):
    if scratch is not None:
        joined, used = [], 0
        for ref, bias in chunks:
            if ref.shape[0] == ROWS:
                joined.append((ref, bias))
            else:
                scratch[used : used + 256, :] = ref[...]
                used += 256
                if used == ROWS:
                    joined.append((scratch, bias))
        chunks = joined
    top_out, acc_out = state_out
    lane = lax.broadcasted_iota(jnp.int32, (1, 128), 1)
    steps = [(head, at) for head in range(HEADS) for at in range(0, ROWS, QB)]

    def scores(step):
        head, at = step
        qh = q[at : at + QB, :] * head_mask(head, HEAD_DIM**-0.5)
        return [dot_nt(qh, ref[:, :FEAT]) for ref, _ in chunks]

    pending = scores(steps[0])
    values = None
    for index, (head, at) in enumerate(steps):
        now = pending
        if index + 1 < len(steps):
            pending = scores(steps[index + 1])
        if at == 0:
            side = 128 * (head // 2)
            own = (lane // HEAD_DIM) == (head % 2)
            values = [
                jnp.where(own, ref[:, FEAT + side : FEAT + side + 128].astype(F32), 1.0).astype(BF16)
                for ref, _ in chunks
            ]
        top = None
        for s, (_, bias) in zip(now, chunks):
            one = jnp.max(s, axis=1, keepdims=True) + bias
            top = one if top is None else jnp.maximum(top, one)
        rows = pl.ds(at, QB)
        if state_in is not None:
            old = state_in[0][rows, head : head + 1]
            top = jnp.maximum(old, top)
            acc = state_in[1][head, rows, :] * jnp.exp(old - top)
        else:
            acc = None
        for s, (ref, bias), vh in zip(now, chunks, values):
            p = jnp.exp(s + (bias - top)).astype(BF16)
            add = dot(p, vh)
            acc = add if acc is None else acc + add
        top_out[rows, head : head + 1] = top
        acc_out[head, rows, :] = acc


def forward_body(biases, has_state, *refs):
    n = len(biases)
    q_ref, chunks, rest = refs[0], refs[1 : 1 + n], refs[1 + n :]
    state_in = rest[:2] if has_state else None
    state_out = rest[2:4] if has_state else rest[:2]
    forward_blocks(q_ref, list(zip(chunks, biases)), state_in, state_out, refs[-1])


def run_forward(q, chunks, biases, state, name, deps=(), token=False, us=LIGHT):
    args = [q, *chunks] + ([] if state is None else list(state))
    keys = sum(c.shape[0] for c in chunks)
    count = len(args)
    outs = [((ROWS, 8), F32), ((HEADS, ROWS, 128), F32)]
    if token:
        outs.append(TOKEN)

    def body(*refs):
        if token:
            refs[count + 2][...] = jnp.zeros(TOKEN[0], TOKEN[1])
            refs = refs[: count + 2] + refs[count + 3 :]
        forward_body(biases, state is not None, *refs)

    return call(
        body,
        outs,
        args,
        name,
        us=us,
        scratch=[pltpu.VMEM((ROWS, PAIR), BF16)],
        deps=deps,
    )


def grad_in_body(og_ref, w_ref, kv_ref, d_ref, out_ref):
    out_ref[...] = kv_ref[...]
    d_ref[...] = dot_nt(og_ref[...], w_ref[...]).astype(BF16)


def finish_body(biases, *refs):
    n = len(biases)
    q_ref, chunks, rest = refs[0], refs[1 : 1 + n], refs[1 + n :]
    top_in, acc_in, d_ref, att_ref, stat_ref, top_s, acc_s, kvs = rest
    forward_blocks(q_ref, list(zip(chunks, biases)), (top_in, acc_in), (top_s, acc_s), kvs)
    lane = lax.broadcasted_iota(jnp.int32, (1, 128), 1)
    logs = jnp.zeros((ROWS, 128), F32)
    products = []
    for side in range(2):
        halves = []
        for odd in range(2):
            head = 2 * side + odd
            acc = acc_s[head]
            halves.append(acc / pltpu.roll(acc, HEAD_DIM, 1))
            at = HEAD_DIM * (1 - odd) + side
            logs = jnp.where(lane == at, top_s[:, head : head + 1] + jnp.log(acc), logs)
        att = jnp.where(lane < HEAD_DIM, halves[0], halves[1]).astype(BF16)
        cols = slice(128 * side, 128 * side + 128)
        att_ref[:, cols] = att
        products.append(d_ref[:, cols].astype(F32) * att.astype(F32))
    flipped = logs.T
    for side in range(2):
        for odd in range(2):
            at = HEAD_DIM * (1 - odd) + side
            head = 2 * side + odd
            stat_ref[head : head + 1, :] = flipped[at : at + 1, :]
    product = jnp.concatenate(products, axis=1)
    high = product.astype(BF16)
    low = (product - high.astype(F32)).astype(BF16)
    row = lax.broadcasted_iota(jnp.int32, (16, FEAT), 0)
    col = lax.broadcasted_iota(jnp.int32, (16, FEAT), 1)
    pick = jnp.where(col // HEAD_DIM == row, 1.0, 0.0).astype(BF16)
    delta = dot_nt(pick, high) + dot_nt(pick, low)
    stat_ref[HEADS : 2 * HEADS, :] = delta[:HEADS, :]


def run_finish(q, chunks, biases, state, d):
    keys = sum(c.shape[0] for c in chunks)
    return call(
        lambda *refs: finish_body(biases, *refs),
        [((ROWS, FEAT), BF16), ((8, ROWS), F32)],
        [q, *chunks, *state, d],
        "finish",
        us=LIGHT,
        scratch=[
            pltpu.VMEM((ROWS, 8), F32),
            pltpu.VMEM((HEADS, ROWS, 128), F32),
            pltpu.VMEM((ROWS, PAIR), BF16),
        ],
    )


def backward_body(biases, has_acc, last, joined, *refs):
    n = len(biases)
    q_ref, d_ref, stat_ref = refs[:3]
    chunks = refs[3 : 3 + n]
    rest = refs[3 + n :]
    acc_in = rest[0] if has_acc else None
    rest = rest[1:] if has_acc else rest
    m = n - 1 if joined else n
    outs, dq_ref, qs, ds, ps, gs, kvs = rest[:m], rest[m], *rest[m + 1 :]
    if joined:
        outs = (*outs, outs[-1])
    q, d = q_ref[...], d_ref[...]
    for head in range(HEADS):
        qs[pl.ds(head * ROWS, ROWS), :] = q * head_mask(head, HEAD_DIM**-0.5)
        ds[pl.ds(head * ROWS, ROWS), :] = d * head_mask(head, 1.0)
    blocks, flat, used = [], [], 0
    for ref, bias, out in zip(chunks, biases, outs):
        if ref.shape[0] == ROWS:
            blocks.append((ref, bias, [(out, 0)]))
        else:
            kvs[used : used + 256, :] = ref[...]
            flat = [(out, 0)] if joined else flat + [(out, used)]
            used += 256
            if used == ROWS:
                blocks.append((kvs, bias, flat))
    pieces = [None] * HEADS
    for ref, bias, parts in blocks:
        for head in range(HEADS):
            at = pl.ds(head * ROWS, ROWS)
            shift = bias - stat_ref[head : head + 1, :]
            delta = stat_ref[HEADS + head : HEADS + head + 1, :]
            p = jnp.exp(dot_nt(ref[:, :FEAT], qs[at, :]) + shift).astype(BF16)
            ps[:, at] = p
            gs[:, at] = p * (dot_nt(ref[:, FEAT:], ds[at, :]) - delta).astype(BF16)
        dk = dot(gs[...], qs[...]).astype(BF16)
        dv = dot(ps[...], ds[...]).astype(BF16)
        for out, start in parts:
            rows = slice(start, start + out.shape[0])
            out[:, :FEAT] = dk[rows, :]
            out[:, FEAT:] = dv[rows, :]
        flipped = ref[:, :FEAT].T
        for head in range(HEADS):
            part = dot(
                flipped[head * HEAD_DIM : (head + 1) * HEAD_DIM, :],
                gs[:, head * ROWS : (head + 1) * ROWS],
            )
            pieces[head] = part if pieces[head] is None else pieces[head] + part
    total = jnp.concatenate(pieces, axis=0) * HEAD_DIM**-0.5
    if acc_in is not None:
        total = total + acc_in[...]
    dq_ref[...] = total.T.astype(BF16) if last else total


def run_backward(q, d, stat, chunks, biases, acc, name, last=False, joined=False, deps=(), us=LIGHT):
    args = [q, d, stat, *chunks] + ([] if acc is None else [acc])
    keys = sum(c.shape[0] for c in chunks)
    outs = [((c.shape[0], PAIR), BF16) for c in chunks]
    if joined:
        outs = outs[:-2] + [((ROWS, PAIR), BF16)]
    outs.append(((ROWS, FEAT), BF16) if last else ((FEAT, ROWS), F32))
    return call(
        lambda *refs: backward_body(biases, acc is not None, last, joined, *refs),
        outs,
        args,
        name,
        us=us,
        deps=deps,
        scratch=[
            pltpu.VMEM((HEADS * ROWS, FEAT), BF16),
            pltpu.VMEM((HEADS * ROWS, FEAT), BF16),
            pltpu.VMEM((ROWS, HEADS * ROWS), BF16),
            pltpu.VMEM((ROWS, HEADS * ROWS), BF16),
            pltpu.VMEM((ROWS, PAIR), BF16),
        ],
    )


def own_part(place_ref, mask):
    at = jnp.bitwise_xor(place_ref[0], mask) * 128
    return pl.ds(pl.multiple_of(at, 128), 128)


def spread2(x):
    return dot(spread_matrix(x.shape[0], 2, 0.5), x.astype(BF16))


def spread4(x):
    return dot(spread_matrix(x.shape[0], 4, 0.25), x.astype(BF16))


def pass_on(place_ref, total_ref, grads, keep_ref, o1_ref, o2_ref, o3_ref):
    keep_ref[...] = total_ref[own_part(place_ref, 0), :]
    o1_ref[...] = total_ref[own_part(place_ref, 1), :].astype(BF16)
    for mask, grad, out in ((2, grads[0], o2_ref), (3, grads[1], o3_ref)):
        below = total_ref[own_part(place_ref, mask), :]
        out[...] = (grad.astype(F32) + spread2(below)).astype(BF16)


def home_far_body(
    place_ref, r_ref, ra_ref, rb_ref, g2_ref, g3_ref, keep_ref, o1_ref, o2_ref, o3_ref, total_ref
):
    total_ref[...] = r_ref[...].astype(F32) + spread2(ra_ref[...]) + spread2(rb_ref[...])
    pass_on(
        place_ref, total_ref, (g2_ref[...], g3_ref[...]), keep_ref, o1_ref, o2_ref, o3_ref
    )


def coarse_total(r_ref, r2_ref, r3_ref, kept_ref, e1_ref):
    below = kept_ref[...] + e1_ref[...].astype(F32)
    total = r_ref[...].astype(F32) + spread2(r2_ref[...]) + spread2(r3_ref[...])
    return total + spread4(below)


def home_mid_body(
    place_ref, r_ref, r2_ref, r3_ref, kept_ref, e1_ref, g_ref,
    keep_ref, o1_ref, o2_ref, o3_ref, total_ref,
):
    total_ref[...] = coarse_total(r_ref, r2_ref, r3_ref, kept_ref, e1_ref)
    pass_on(
        place_ref, total_ref, (g_ref[256:, :], g_ref[:256, :]), keep_ref, o1_ref, o2_ref, o3_ref
    )


def home_near_body(r_ref, r2_ref, r3_ref, kept_ref, e1_ref, g_ref, dk_ref, dv_ref):
    total = coarse_total(r_ref, r2_ref, r3_ref, kept_ref, e1_ref) + g_ref[...].astype(F32)
    dk_ref[...] = total[:, :FEAT].astype(BF16)
    dv_ref[...] = total[:, FEAT:].astype(BF16)


def mixed_send_body(side_ref, att_ref, w_ref, out_ref):
    at = pl.multiple_of((1 - side_ref[0]) * PAIR, PAIR)
    out_ref[...] = dot(att_ref[...], w_ref[:, pl.ds(at, PAIR)]).astype(BF16)


def mixed_sum_body(side_ref, att_ref, w_ref, got_ref, out_ref, token_ref):
    token_ref[...] = jnp.zeros(TOKEN[0], TOKEN[1])
    at = pl.multiple_of(side_ref[0] * PAIR, PAIR)
    own = dot(att_ref[...], w_ref[:, pl.ds(at, PAIR)])
    out_ref[...] = (own + got_ref[...].astype(F32)).astype(BF16)


def swap(value, mask):
    return lax.ppermute(value, "seq", [(s, s ^ mask) for s in range(lax.axis_size("seq"))])


def per_device(queries, key_vectors, value_vectors, out_weight, out_grad):
    place = lax.axis_index("seq").astype(jnp.int32)
    side = lax.axis_index("head").astype(jnp.int32).reshape(1)
    place_z = jnp.bitwise_and(place, 3).reshape(1)
    place_x = jnp.bitwise_and(jnp.right_shift(place, 2), 3).reshape(1)
    bias = [max(level - 1, 0) * LN2 for level in range(7)]
    wide, half, part = ((ROWS, PAIR), BF16), ((256, PAIR), BF16), ((128, PAIR), BF16)
    kept = ((128, PAIR), F32)
    whole = pltpu.VMEM((ROWS, PAIR), F32)

    kv, c2, c3 = call(
        prep_body, [wide, half, part], [key_vectors, value_vectors], "prep", us=LIGHT,
        scratch=[pltpu.SemaphoreType.DMA((2,))], far=(0, 1), limit=60 * 1024 * 1024,
    )
    s1, s3, s2 = swap(c3, 1), swap(c3, 3), swap(c3, 2)
    d, kv_z = call(
        grad_in_body, [((ROWS, FEAT), BF16), wide], [out_grad, out_weight, kv], "grad_in",
        us=LIGHT, deps=[s1],
    )
    p1 = swap(kv_z, 1)
    own3, c4, c5 = call(
        gather_body, [wide, half, part], [place_z, c3, s1, s2, s3], "gather_z", us=HEAVY,
        smem=(0,), deps=[kv_z],
    )
    p3, p4a, p4b = swap(own3, 4), swap(c4, 12), swap(c4, 8)
    *state, token = run_forward(queries, [kv], [bias[0]], None, "fwd0", token=True, deps=[c5])
    own5, c6 = call(
        gather_far_body, [wide, half], [place_x, c5, p3, p4b, p4a], "gather_x", us=HEAVY,
        smem=(0,), deps=[token],
    )
    p5, p6a, p6b = swap(own5, 16), swap(c6, 48), swap(c6, 32)
    own2 = call(join_body, [wide], [c2, p1], "join2", us=LIGHT)[0]
    p2 = swap(own2, 3)
    state = run_forward(queries, [p1, p2], [bias[1], bias[2]], state, "fwd12")
    state = run_forward(queries, [p3, p4a, p4b], [bias[3], bias[4], bias[4]], state, "fwd34")
    att, stat = run_finish(queries, [p5, p6a, p6b], [bias[5], bias[6], bias[6]], state, d)

    def back(chunks, levels, acc, name, **more):
        return run_backward(
            queries, d, stat, chunks, [bias[level] for level in levels], acc, name, **more
        )

    g5, g6a, g6b, dq = back([p5, p6a, p6b], [5, 6, 6], None, "bwd56")
    r5, r6a, r6b = swap(g5, 16), swap(g6a, 48), swap(g6b, 32)
    g3, dq = back([p3], [3], dq, "bwd3")
    r3 = swap(g3, 4)
    g4a, g4b, g1, g2, dq = back([p4a, p4b, p1, p2], [4, 4, 1, 2], dq, "bwd124")
    r1 = swap(g1, 1)
    k5, e1, e2, e3 = call(
        home_far_body, [kept, part, half, half], [place_x, r5, r6a, r6b, g4b, g4a], "home_far",
        us=HEAVY, scratch=[whole], smem=(0,), deps=[g1],
    )
    e3, e2, e1 = swap(e3, 12), swap(e2, 8), swap(e1, 4)
    g0, query_grads = back([kv], [0], dq, "bwd0", last=True, deps=[k5])
    mixed_out = call(
        mixed_send_body, [wide], [side, att, out_weight], "mixed_send", us=LIGHT, smem=(0,),
        deps=[g0],
    )[0]
    mixed_in = lax.ppermute(mixed_out, "head", [(0, 1), (1, 0)])
    k3, f1, f2, f3 = call(
        home_mid_body, [kept, part, half, half], [place_z, r3, e2, e3, k5, e1, g2], "home_mid",
        us=HEAVY, scratch=[whole], smem=(0,), deps=[g0, r1],
    )
    f3, f2, f1 = swap(f3, 3), swap(f2, 2), swap(f1, 1)
    mixed, token = call(
        mixed_sum_body, [wide, TOKEN], [side, att, out_weight, mixed_in], "mixed_sum", us=LIGHT,
        smem=(0,), deps=[k3],
    )
    key_grads, value_grads = call(
        home_near_body, [((ROWS, FEAT), BF16)] * 2, [r1, f2, f3, k3, f1, g0], "home_near",
        us=LIGHT, deps=[token],
    )
    return (mixed, query_grads, key_grads, value_grads)


def solution(mesh):
    return jax.shard_map(
        per_device,
        mesh=mesh,
        in_specs=(
            P("seq", "head"),
            P("seq", "head"),
            P("seq", "head"),
            P("head", None),
            P("seq", None),
        ),
        out_specs=(P("seq", "head"), P("seq", "head"), P("seq", "head"), P("seq", "head")),
        check_vma=False,
    )
```

```python
import math

import jax
import jax.numpy as jnp
from jax import lax
from jax.experimental import pallas as pl
from jax.experimental.pallas import tpu as pltpu
from jax.sharding import PartitionSpec as P

HEAD_DIM = 64
ROWS = 512
FEAT = 256
HEADS = 4
PAIR = 2 * FEAT
LN2 = math.log(2.0)
F32 = jnp.float32
BF16 = jnp.bfloat16
QB = 512
NT = (((1,), (1,)), ((), ()))
VMEM_LIMIT = 20 * 1024 * 1024
SCALE = 1.0
LIGHT = 0.01
HEAVY = 60.0
TOKEN = ((8, 128), jnp.float32)


def call(body, outs, args, name, us, scratch=(), smem=(), far=(), deps=(), limit=VMEM_LIMIT):
    count = len(args)

    def run(*refs):
        body(*refs[:count], *refs[count + len(deps) :])

    def space(i):
        return pltpu.SMEM if i in smem else pl.ANY if i in far else pltpu.VMEM

    return pl.pallas_call(
        run,
        out_shape=[jax.ShapeDtypeStruct(s, t) for s, t in outs],
        in_specs=[pl.BlockSpec(memory_space=space(i)) for i in range(count)]
        + [pl.BlockSpec(memory_space=pl.ANY)] * len(deps),
        out_specs=[pl.BlockSpec(memory_space=pltpu.VMEM) for _ in outs],
        scratch_shapes=list(scratch),
        compiler_params=pltpu.CompilerParams(vmem_limit_bytes=limit),
        cost_estimate=pl.CostEstimate(
            flops=int(us * SCALE * 1.1e9), bytes_accessed=1 << 16, transcendentals=0
        ),
        name=name,
    )(*args, *deps)


def dot(a, b):
    return jnp.dot(a, b, preferred_element_type=F32)


def dot_nt(a, b):
    return lax.dot_general(a, b, NT, preferred_element_type=F32)


def pair_matrix(rows, fold, weight):
    r = lax.broadcasted_iota(jnp.int32, (rows, rows * fold), 0)
    c = lax.broadcasted_iota(jnp.int32, (rows, rows * fold), 1)
    return jnp.where(c // fold == r, weight, 0.0).astype(BF16)


def spread_matrix(rows, fold, weight):
    r = lax.broadcasted_iota(jnp.int32, (rows * fold, rows), 0)
    c = lax.broadcasted_iota(jnp.int32, (rows * fold, rows), 1)
    return jnp.where(r // fold == c, weight, 0.0).astype(BF16)


def halve(x):
    return dot(pair_matrix(x.shape[0] // 2, 2, 0.5), x).astype(BF16)


def head_mask(head, value):
    lane = lax.broadcasted_iota(jnp.int32, (1, FEAT), 1)
    return jnp.where(lane // HEAD_DIM == head, value, 0.0).astype(BF16)


def prep_body(k_ref, v_ref, kv_ref, c2_ref, c3_ref, sems):
    copies = [
        pltpu.make_async_copy(k_ref, kv_ref.at[:, pl.ds(0, FEAT)], sems.at[0]),
        pltpu.make_async_copy(v_ref, kv_ref.at[:, pl.ds(FEAT, FEAT)], sems.at[1]),
    ]
    for copy in copies:
        copy.start()
    for copy in copies:
        copy.wait()
    c2_ref[...] = halve(kv_ref[...])
    c3_ref[...] = halve(c2_ref[...])


def join_body(own_ref, got_ref, out_ref):
    out_ref[:256, :] = own_ref[...]
    out_ref[256:, :] = halve(got_ref[...])


def gather_body(place_ref, own_ref, a_ref, b_ref, c_ref, whole_ref, half_ref, quarter_ref=None):
    place = place_ref[0]
    for mask, ref in ((0, own_ref), (1, a_ref), (2, b_ref), (3, c_ref)):
        at = pl.multiple_of(jnp.bitwise_xor(place, mask) * 128, 128)
        whole_ref[pl.ds(at, 128), :] = ref[...]
    half_ref[...] = halve(whole_ref[...])
    if quarter_ref is not None:
        quarter_ref[...] = halve(half_ref[...])


def gather_far_body(place_ref, own_ref, a_ref, b_ref, c_ref, whole_ref, half_ref):
    for mask, rows in (
        (0, own_ref[...]),
        (1, halve(halve(a_ref[...]))),
        (2, halve(b_ref[...])),
        (3, halve(c_ref[...])),
    ):
        at = jnp.bitwise_xor(place_ref[0], mask) * 128
        whole_ref[pl.ds(pl.multiple_of(at, 128), 128), :] = rows
    half_ref[...] = halve(whole_ref[...])


def forward_blocks(q, chunks, state_in, state_out, scratch=None):
    if scratch is not None:
        joined, used = [], 0
        for ref, bias in chunks:
            if ref.shape[0] == ROWS:
                joined.append((ref, bias))
            else:
                scratch[used : used + 256, :] = ref[...]
                used += 256
                if used == ROWS:
                    joined.append((scratch, bias))
        chunks = joined
    top_out, acc_out = state_out
    lane = lax.broadcasted_iota(jnp.int32, (1, 128), 1)
    steps = [(head, at) for head in range(HEADS) for at in range(0, ROWS, QB)]

    def scores(step):
        head, at = step
        qh = q[at : at + QB, :] * head_mask(head, HEAD_DIM**-0.5)
        return [dot_nt(qh, ref[:, :FEAT]) for ref, _ in chunks]

    pending = scores(steps[0])
    values = None
    for index, (head, at) in enumerate(steps):
        now = pending
        if index + 1 < len(steps):
            pending = scores(steps[index + 1])
        if at == 0:
            side = 128 * (head // 2)
            own = (lane // HEAD_DIM) == (head % 2)
            values = [
                jnp.where(own, ref[:, FEAT + side : FEAT + side + 128].astype(F32), 1.0).astype(BF16)
                for ref, _ in chunks
            ]
        top = None
        for s, (_, bias) in zip(now, chunks):
            one = jnp.max(s, axis=1, keepdims=True) + bias
            top = one if top is None else jnp.maximum(top, one)
        rows = pl.ds(at, QB)
        if state_in is not None:
            old = state_in[0][rows, head : head + 1]
            top = jnp.maximum(old, top)
            acc = state_in[1][head, rows, :] * jnp.exp(old - top)
        else:
            acc = None
        for s, (ref, bias), vh in zip(now, chunks, values):
            p = jnp.exp(s + (bias - top)).astype(BF16)
            add = dot(p, vh)
            acc = add if acc is None else acc + add
        top_out[rows, head : head + 1] = top
        acc_out[head, rows, :] = acc


def forward_body(biases, has_state, *refs):
    n = len(biases)
    q_ref, chunks, rest = refs[0], refs[1 : 1 + n], refs[1 + n :]
    state_in = rest[:2] if has_state else None
    state_out = rest[2:4] if has_state else rest[:2]
    forward_blocks(q_ref, list(zip(chunks, biases)), state_in, state_out, refs[-1])


def run_forward(q, chunks, biases, state, name, deps=(), token=False, us=LIGHT):
    args = [q, *chunks] + ([] if state is None else list(state))
    keys = sum(c.shape[0] for c in chunks)
    count = len(args)
    outs = [((ROWS, 8), F32), ((HEADS, ROWS, 128), F32)]
    if token:
        outs.append(TOKEN)

    def body(*refs):
        if token:
            refs[count + 2][...] = jnp.zeros(TOKEN[0], TOKEN[1])
            refs = refs[: count + 2] + refs[count + 3 :]
        forward_body(biases, state is not None, *refs)

    return call(
        body,
        outs,
        args,
        name,
        us=us,
        scratch=[pltpu.VMEM((ROWS, PAIR), BF16)],
        deps=deps,
    )


def grad_in_body(og_ref, w_ref, kv_ref, d_ref, out_ref):
    out_ref[...] = kv_ref[...]
    d_ref[...] = dot_nt(og_ref[...], w_ref[...]).astype(BF16)


def finish_body(biases, *refs):
    n = len(biases)
    q_ref, chunks, rest = refs[0], refs[1 : 1 + n], refs[1 + n :]
    top_in, acc_in, d_ref, att_ref, stat_ref, top_s, acc_s, kvs = rest
    forward_blocks(q_ref, list(zip(chunks, biases)), (top_in, acc_in), (top_s, acc_s), kvs)
    lane = lax.broadcasted_iota(jnp.int32, (1, 128), 1)
    logs = jnp.zeros((ROWS, 128), F32)
    products = []
    for side in range(2):
        halves = []
        for odd in range(2):
            head = 2 * side + odd
            acc = acc_s[head]
            halves.append(acc / pltpu.roll(acc, HEAD_DIM, 1))
            at = HEAD_DIM * (1 - odd) + side
            logs = jnp.where(lane == at, top_s[:, head : head + 1] + jnp.log(acc), logs)
        att = jnp.where(lane < HEAD_DIM, halves[0], halves[1]).astype(BF16)
        cols = slice(128 * side, 128 * side + 128)
        att_ref[:, cols] = att
        products.append(d_ref[:, cols].astype(F32) * att.astype(F32))
    flipped = logs.T
    for side in range(2):
        for odd in range(2):
            at = HEAD_DIM * (1 - odd) + side
            head = 2 * side + odd
            stat_ref[head : head + 1, :] = flipped[at : at + 1, :]
    product = jnp.concatenate(products, axis=1)
    high = product.astype(BF16)
    low = (product - high.astype(F32)).astype(BF16)
    row = lax.broadcasted_iota(jnp.int32, (16, FEAT), 0)
    col = lax.broadcasted_iota(jnp.int32, (16, FEAT), 1)
    pick = jnp.where(col // HEAD_DIM == row, 1.0, 0.0).astype(BF16)
    delta = dot_nt(pick, high) + dot_nt(pick, low)
    stat_ref[HEADS : 2 * HEADS, :] = delta[:HEADS, :]


def run_finish(q, chunks, biases, state, d):
    keys = sum(c.shape[0] for c in chunks)
    return call(
        lambda *refs: finish_body(biases, *refs),
        [((ROWS, FEAT), BF16), ((8, ROWS), F32)],
        [q, *chunks, *state, d],
        "finish",
        us=LIGHT,
        scratch=[
            pltpu.VMEM((ROWS, 8), F32),
            pltpu.VMEM((HEADS, ROWS, 128), F32),
            pltpu.VMEM((ROWS, PAIR), BF16),
        ],
    )


def backward_body(biases, has_acc, last, joined, *refs):
    n = len(biases)
    q_ref, d_ref, stat_ref = refs[:3]
    chunks = refs[3 : 3 + n]
    rest = refs[3 + n :]
    acc_in = rest[0] if has_acc else None
    rest = rest[1:] if has_acc else rest
    m = n - 1 if joined else n
    outs, dq_ref, qs, ds, ps, gs, kvs = rest[:m], rest[m], *rest[m + 1 :]
    if joined:
        outs = (*outs, outs[-1])
    q, d = q_ref[...], d_ref[...]
    for head in range(HEADS):
        qs[pl.ds(head * ROWS, ROWS), :] = q * head_mask(head, HEAD_DIM**-0.5)
        ds[pl.ds(head * ROWS, ROWS), :] = d * head_mask(head, 1.0)
    blocks, flat, used = [], [], 0
    for ref, bias, out in zip(chunks, biases, outs):
        if ref.shape[0] == ROWS:
            blocks.append((ref, bias, [(out, 0)]))
        else:
            kvs[used : used + 256, :] = ref[...]
            flat = [(out, 0)] if joined else flat + [(out, used)]
            used += 256
            if used == ROWS:
                blocks.append((kvs, bias, flat))
    pieces = [None] * HEADS
    for ref, bias, parts in blocks:
        for head in range(HEADS):
            at = pl.ds(head * ROWS, ROWS)
            shift = bias - stat_ref[head : head + 1, :]
            delta = stat_ref[HEADS + head : HEADS + head + 1, :]
            p = jnp.exp(dot_nt(ref[:, :FEAT], qs[at, :]) + shift).astype(BF16)
            ps[:, at] = p
            gs[:, at] = p * (dot_nt(ref[:, FEAT:], ds[at, :]) - delta).astype(BF16)
        dk = dot(gs[...], qs[...]).astype(BF16)
        dv = dot(ps[...], ds[...]).astype(BF16)
        for out, start in parts:
            rows = slice(start, start + out.shape[0])
            out[:, :FEAT] = dk[rows, :]
            out[:, FEAT:] = dv[rows, :]
        flipped = ref[:, :FEAT].T
        for head in range(HEADS):
            part = dot(
                flipped[head * HEAD_DIM : (head + 1) * HEAD_DIM, :],
                gs[:, head * ROWS : (head + 1) * ROWS],
            )
            pieces[head] = part if pieces[head] is None else pieces[head] + part
    total = jnp.concatenate(pieces, axis=0) * HEAD_DIM**-0.5
    if acc_in is not None:
        total = total + acc_in[...]
    dq_ref[...] = total.T.astype(BF16) if last else total


def run_backward(q, d, stat, chunks, biases, acc, name, last=False, joined=False, deps=(), us=LIGHT):
    args = [q, d, stat, *chunks] + ([] if acc is None else [acc])
    keys = sum(c.shape[0] for c in chunks)
    outs = [((c.shape[0], PAIR), BF16) for c in chunks]
    if joined:
        outs = outs[:-2] + [((ROWS, PAIR), BF16)]
    outs.append(((ROWS, FEAT), BF16) if last else ((FEAT, ROWS), F32))
    return call(
        lambda *refs: backward_body(biases, acc is not None, last, joined, *refs),
        outs,
        args,
        name,
        us=us,
        deps=deps,
        scratch=[
            pltpu.VMEM((HEADS * ROWS, FEAT), BF16),
            pltpu.VMEM((HEADS * ROWS, FEAT), BF16),
            pltpu.VMEM((ROWS, HEADS * ROWS), BF16),
            pltpu.VMEM((ROWS, HEADS * ROWS), BF16),
            pltpu.VMEM((ROWS, PAIR), BF16),
        ],
    )


def own_part(place_ref, mask):
    at = jnp.bitwise_xor(place_ref[0], mask) * 128
    return pl.ds(pl.multiple_of(at, 128), 128)


def spread2(x):
    return dot(spread_matrix(x.shape[0], 2, 0.5), x.astype(BF16))


def spread4(x):
    return dot(spread_matrix(x.shape[0], 4, 0.25), x.astype(BF16))


def pass_on(place_ref, total_ref, grads, keep_ref, o1_ref, o2_ref, o3_ref):
    keep_ref[...] = total_ref[own_part(place_ref, 0), :]
    o1_ref[...] = total_ref[own_part(place_ref, 1), :].astype(BF16)
    for mask, grad, out in ((2, grads[0], o2_ref), (3, grads[1], o3_ref)):
        below = total_ref[own_part(place_ref, mask), :]
        out[...] = (grad.astype(F32) + spread2(below)).astype(BF16)


def home_far_body(
    place_ref, r_ref, ra_ref, rb_ref, g2_ref, g3_ref, keep_ref, o1_ref, o2_ref, o3_ref, total_ref
):
    finer = ra_ref[...].astype(F32) + rb_ref[...].astype(F32)
    total_ref[...] = r_ref[...].astype(F32) + spread2(finer)
    pass_on(
        place_ref, total_ref, (g2_ref[...], g3_ref[...]), keep_ref, o1_ref, o2_ref, o3_ref
    )


def coarse_total(r_ref, r2_ref, r3_ref, kept_ref, e1_ref):
    below = kept_ref[...] + e1_ref[...].astype(F32)
    finer = r2_ref[...].astype(F32) + r3_ref[...].astype(F32)
    return r_ref[...].astype(F32) + spread2(finer) + spread4(below)


def home_mid_body(
    place_ref, r_ref, r2_ref, r3_ref, kept_ref, e1_ref, g_ref,
    keep_ref, o1_ref, o2_ref, o3_ref, total_ref,
):
    total_ref[...] = coarse_total(r_ref, r2_ref, r3_ref, kept_ref, e1_ref)
    pass_on(
        place_ref, total_ref, (g_ref[256:, :], g_ref[:256, :]), keep_ref, o1_ref, o2_ref, o3_ref
    )


def home_near_body(r_ref, r2_ref, r3_ref, kept_ref, e1_ref, g_ref, dk_ref, dv_ref):
    total = coarse_total(r_ref, r2_ref, r3_ref, kept_ref, e1_ref) + g_ref[...].astype(F32)
    dk_ref[...] = total[:, :FEAT].astype(BF16)
    dv_ref[...] = total[:, FEAT:].astype(BF16)


def mixed_send_body(side_ref, att_ref, w_ref, out_ref):
    at = pl.multiple_of((1 - side_ref[0]) * PAIR, PAIR)
    out_ref[...] = dot(att_ref[...], w_ref[:, pl.ds(at, PAIR)]).astype(BF16)


def mixed_sum_body(side_ref, att_ref, w_ref, got_ref, out_ref, token_ref):
    token_ref[...] = jnp.zeros(TOKEN[0], TOKEN[1])
    at = pl.multiple_of(side_ref[0] * PAIR, PAIR)
    own = dot(att_ref[...], w_ref[:, pl.ds(at, PAIR)])
    out_ref[...] = (own + got_ref[...].astype(F32)).astype(BF16)


def swap(value, mask):
    return lax.ppermute(value, "seq", [(s, s ^ mask) for s in range(lax.axis_size("seq"))])


def per_device(queries, key_vectors, value_vectors, out_weight, out_grad):
    place = lax.axis_index("seq").astype(jnp.int32)
    side = lax.axis_index("head").astype(jnp.int32).reshape(1)
    place_z = jnp.bitwise_and(place, 3).reshape(1)
    place_x = jnp.bitwise_and(jnp.right_shift(place, 2), 3).reshape(1)
    bias = [max(level - 1, 0) * LN2 for level in range(7)]
    wide, half, part = ((ROWS, PAIR), BF16), ((256, PAIR), BF16), ((128, PAIR), BF16)
    kept = ((128, PAIR), F32)
    whole = pltpu.VMEM((ROWS, PAIR), F32)

    kv, c2, c3 = call(
        prep_body, [wide, half, part], [key_vectors, value_vectors], "prep", us=LIGHT,
        scratch=[pltpu.SemaphoreType.DMA((2,))], far=(0, 1), limit=60 * 1024 * 1024,
    )
    s1, s3, s2 = swap(c3, 1), swap(c3, 3), swap(c3, 2)
    d, kv_z = call(
        grad_in_body, [((ROWS, FEAT), BF16), wide], [out_grad, out_weight, kv], "grad_in",
        us=LIGHT, deps=[s1],
    )
    p1 = swap(kv_z, 1)
    own3, c4, c5 = call(
        gather_body, [wide, half, part], [place_z, c3, s1, s2, s3], "gather_z", us=HEAVY,
        smem=(0,), deps=[kv_z],
    )
    p3, p4a, p4b = swap(own3, 4), swap(c4, 12), swap(c4, 8)
    *state, token = run_forward(queries, [kv], [bias[0]], None, "fwd0", token=True, deps=[c5])
    own5, c6 = call(
        gather_far_body, [wide, half], [place_x, c5, p3, p4b, p4a], "gather_x", us=HEAVY,
        smem=(0,), deps=[token],
    )
    p5, p6a, p6b = swap(own5, 16), swap(c6, 48), swap(c6, 32)
    own2 = call(join_body, [wide], [c2, p1], "join2", us=LIGHT)[0]
    p2 = swap(own2, 3)
    state = run_forward(queries, [p1, p2], [bias[1], bias[2]], state, "fwd12")
    state = run_forward(queries, [p3, p4a, p4b], [bias[3], bias[4], bias[4]], state, "fwd34")
    att, stat = run_finish(queries, [p5, p6a, p6b], [bias[5], bias[6], bias[6]], state, d)

    def back(chunks, levels, acc, name, **more):
        return run_backward(
            queries, d, stat, chunks, [bias[level] for level in levels], acc, name, **more
        )

    g5, g6a, g6b, dq = back([p5, p6a, p6b], [5, 6, 6], None, "bwd56")
    r5, r6a, r6b = swap(g5, 16), swap(g6a, 48), swap(g6b, 32)
    g3, dq = back([p3], [3], dq, "bwd3")
    r3 = swap(g3, 4)
    g4a, g4b, g1, g2, dq = back([p4a, p4b, p1, p2], [4, 4, 1, 2], dq, "bwd124")
    r1 = swap(g1, 1)
    k5, e1, e2, e3 = call(
        home_far_body, [kept, part, half, half], [place_x, r5, r6a, r6b, g4b, g4a], "home_far",
        us=HEAVY, scratch=[whole], smem=(0,), deps=[g1],
    )
    e3, e2, e1 = swap(e3, 12), swap(e2, 8), swap(e1, 4)
    g0, query_grads = back([kv], [0], dq, "bwd0", last=True, deps=[k5])
    mixed_out = call(
        mixed_send_body, [wide], [side, att, out_weight], "mixed_send", us=LIGHT, smem=(0,),
        deps=[g0],
    )[0]
    mixed_in = lax.ppermute(mixed_out, "head", [(0, 1), (1, 0)])
    k3, f1, f2, f3 = call(
        home_mid_body, [kept, part, half, half], [place_z, r3, e2, e3, k5, e1, g2], "home_mid",
        us=HEAVY, scratch=[whole], smem=(0,), deps=[g0, r1],
    )
    f3, f2, f1 = swap(f3, 3), swap(f2, 2), swap(f1, 1)
    mixed, token = call(
        mixed_sum_body, [wide, TOKEN], [side, att, out_weight, mixed_in], "mixed_sum", us=LIGHT,
        smem=(0,), deps=[k3],
    )
    key_grads, value_grads = call(
        home_near_body, [((ROWS, FEAT), BF16)] * 2, [r1, f2, f3, k3, f1, g0], "home_near",
        us=LIGHT, deps=[token],
    )
    return (mixed, query_grads, key_grads, value_grads)


def solution(mesh):
    return jax.shard_map(
        per_device,
        mesh=mesh,
        in_specs=(
            P("seq", "head"),
            P("seq", "head"),
            P("seq", "head"),
            P("head", None),
            P("seq", None),
        ),
        out_specs=(P("seq", "head"), P("seq", "head"), P("seq", "head"), P("seq", "head")),
        check_vma=False,
    )
```
